32 devices in a mesh: dp: 8 (over y, x, core), tensor: 4 (over z).
Axes of the slice: x: 2, y: 2, z: 4, core: 2. Of those that a mesh axis runs over, the one named last changes fastest.
Arguments:
- tokens: bfloat16 [512, 6144], P(('dp', 'tensor')), may hold values from -6 to 6
- router_weight: bfloat16 [6144, 8], replicated, may hold values from -0.078125 to 0.078125
- expert_ids: int32 [512, 2], P(('dp', 'tensor')), may hold values from 0 to 7, as said below
- gate_weight: bfloat16 [6144, 8192], P('dp', 'tensor'), may hold values from -0.078125 to 0.078125
- up_weight: bfloat16 [6144, 8192], P('dp', 'tensor'), may hold values from -0.078125 to 0.078125
Outputs:
- hidden: bfloat16 [512, 8192], P('dp', 'tensor')
The draws below stay inside these ranges and needn't reach their ends.
Inputs may be any that keep to these rules, and one draw needn't show every extreme that they name: `expert_ids`: each row holds two different expert numbers; the share of tokens that name expert 0 varies from one index of dp to another.
All inputs are finite; a program needn't handle non-finite values.
Results may differ from the reference program's by a relative error of at most 0.0046.
Values may be sent and summed in bfloat16 or wider, within the bound.
A program may use at most 128 MiB of HBM per device.

```python
import jax
import jax.numpy as jnp

D = 6144
EXPERTS = 8
FF = 8192
GROUP = 64
TOKENS = 512


def draw_expert_ids(key, part):
    keys = jax.random.split(key, 6)
    groups = TOKENS // GROUP
    level = jax.random.randint(keys[0], (groups,), 1, 6)
    per_row = jnp.repeat(level, GROUP, total_repeat_length=TOKENS)
    roll = jax.random.randint(keys[1], (TOKENS,), 0, EXPERTS)
    routed = roll < per_row
    partner = jax.random.randint(keys[2], (TOKENS,), 1, EXPERTS)
    first = jax.random.randint(keys[3], (TOKENS,), 1, EXPERTS)
    second = 1 + (first - 1 + jax.random.randint(keys[4], (TOKENS,), 1, EXPERTS - 1)) % (EXPERTS - 1)
    flip = jax.random.randint(keys[5], (TOKENS,), 0, 2) == 1
    zeros = jnp.zeros_like(partner)
    left = jnp.where(routed, jnp.where(flip, partner, zeros), first)
    right = jnp.where(routed, jnp.where(flip, zeros, partner), second)
    return jnp.stack([left, right], axis=1).astype(jnp.int32)


def shard_levels(own_key, shape, cuts, low, high):
    def one(position, parts):
        heights = jax.random.uniform(jax.random.fold_in(jax.random.fold_in(own_key, 6), position), (parts,), jnp.float32, low / len(cuts), high / len(cuts))
        return jnp.repeat(jnp.exp(heights), shape[position] // parts).reshape((-1,) + (1,) * (len(shape) - position - 1))

    gain = one(*cuts[0])
    for cut in cuts[1:]:
        gain = gain * one(*cut)
    return gain


def normal_values(own_key, extent, scale, limit, shards=(), held_as=jnp.bfloat16):
    gain = shard_levels(own_key, extent, shards, -0.22, 0.18) if shards else 1.0
    drawn = jax.random.normal(own_key, extent, jnp.float32) * scale * gain
    return jnp.minimum(jnp.maximum(drawn, -limit), limit).astype(held_as)


def setup_inputs(seed: int = 0) -> dict:
    key_of = jax.random.split(jax.random.key(seed), 6)
    tokens = normal_values(key_of[0], (TOKENS, D), 1.0, 6.0, ((0, 32),))
    router_weight = normal_values(key_of[1], (D, EXPERTS), D ** -0.5, 0.078125)
    expert_ids = draw_expert_ids(jax.random.fold_in(key_of[5], 71), 0)
    gate_weight = normal_values(key_of[3], (D, FF), D ** -0.5, 0.078125, ((0, 8), (1, 4)))
    up_weight = normal_values(key_of[4], (D, FF), D ** -0.5, 0.078125, ((0, 8), (1, 4)))
    return dict(tokens=tokens, router_weight=router_weight, expert_ids=expert_ids, gate_weight=gate_weight, up_weight=up_weight)


def reference(tokens, router_weight, expert_ids, gate_weight, up_weight):
    logits = jnp.dot(tokens, router_weight, preferred_element_type=jnp.float32)
    first_zero = expert_ids[:, 0] == 0
    routed = first_zero | (expert_ids[:, 1] == 0)
    other = jnp.where(first_zero, expert_ids[:, 1], expert_ids[:, 0])
    picked = jnp.arange(EXPERTS, dtype=jnp.int32)[None, :] == other[:, None]
    other_logit = jnp.sum(jnp.where(picked, logits, jnp.float32(0.0)), axis=1)
    weight = jnp.where(routed, jax.nn.sigmoid(logits[:, 0] - other_logit), jnp.float32(0.0)).astype(jnp.bfloat16)
    gate = jnp.dot(tokens, gate_weight, preferred_element_type=jnp.float32)
    up = jnp.dot(tokens, up_weight, preferred_element_type=jnp.float32)
    hidden = weight.astype(jnp.float32)[:, None] * jax.nn.silu(gate) * up
    return hidden.astype(jnp.bfloat16)
```

```python
import jax
import jax.numpy as jnp
from jax import lax
from jax.sharding import PartitionSpec as P


def share_of_expert(tokens, router_weight, expert_ids):
    logits = jnp.dot(tokens, router_weight, preferred_element_type=jnp.float32)
    first_zero = expert_ids[:, 0] == 0
    routed = first_zero | (expert_ids[:, 1] == 0)
    other = jnp.where(first_zero, expert_ids[:, 1], expert_ids[:, 0])
    picked = jnp.arange(logits.shape[1], dtype=jnp.int32)[None, :] == other[:, None]
    other_logit = jnp.sum(jnp.where(picked, logits, jnp.float32(0.0)), axis=1)
    return jnp.where(routed, jax.nn.sigmoid(logits[:, 0] - other_logit), jnp.float32(0.0)).astype(
        jnp.bfloat16
    )


def stationary_weights(mesh, tokens, router_weight, expert_ids, gate_weight, up_weight):
    dp, tensor = mesh.shape["dp"], mesh.shape["tensor"]
    rows, depth = tokens.shape[0], gate_weight.shape[0]
    weights = lax.all_gather(
        share_of_expert(tokens, router_weight, expert_ids), "tensor", axis=0, tiled=True
    )
    columns = lax.all_to_all(
        tokens.reshape(rows, dp, depth), "dp", split_axis=1, concat_axis=0, tiled=False
    )
    block = lax.all_gather(columns, "tensor", axis=1, tiled=True).reshape(dp * tensor * rows, depth)

    def summed(weight):
        part = jnp.dot(block, weight, preferred_element_type=jnp.float32).astype(jnp.bfloat16)
        part = part.reshape(dp, tensor * rows, -1)
        got = lax.all_to_all(part, "dp", split_axis=0, concat_axis=0, tiled=False)
        return jnp.sum(got.astype(jnp.float32), axis=0)

    gate, up = summed(gate_weight), summed(up_weight)
    hidden = weights.astype(jnp.float32)[:, None] * jax.nn.silu(gate) * up
    return hidden.astype(jnp.bfloat16)


def solution(mesh):
    def per_device(*args):
        return stationary_weights(mesh, *args)

    return jax.shard_map(
        per_device,
        mesh=mesh,
        in_specs=(
            P(("dp", "tensor"), None),
            P(),
            P(("dp", "tensor"), None),
            P("dp", "tensor"),
            P("dp", "tensor"),
        ),
        out_specs=P("dp", "tensor"),
        check_vma=False,
    )
```

```python
import functools

import jax
import jax.numpy as jnp
from jax import lax
from jax.experimental import pallas as pl
from jax.experimental.pallas import tpu as pltpu
from jax.sharding import PartitionSpec as P

MESH = pl.DeviceIdType.MESH
TILE = 512


def share_of_expert(tokens, router_weight, expert_ids):
    logits = jnp.dot(tokens, router_weight, preferred_element_type=jnp.float32)
    first_zero = expert_ids[:, 0] == 0
    routed = first_zero | (expert_ids[:, 1] == 0)
    other = jnp.where(first_zero, expert_ids[:, 1], expert_ids[:, 0])
    picked = jnp.arange(logits.shape[1], dtype=jnp.int32)[None, :] == other[:, None]
    other_logit = jnp.sum(jnp.where(picked, logits, jnp.float32(0.0)), axis=1)
    return jnp.where(routed, jax.nn.sigmoid(logits[:, 0] - other_logit), jnp.float32(0.0)).astype(
        jnp.bfloat16
    )


def stationary_weights(mesh, tokens, router_weight, expert_ids, gate_weight, up_weight):
    dp, tensor = mesh.shape["dp"], mesh.shape["tensor"]
    rows, depth = tokens.shape[0], gate_weight.shape[0]
    weights = lax.all_gather(
        share_of_expert(tokens, router_weight, expert_ids), "tensor", axis=0, tiled=True
    )
    columns = lax.all_to_all(
        tokens.reshape(rows, dp, depth), "dp", split_axis=1, concat_axis=0, tiled=False
    )
    block = lax.all_gather(columns, "tensor", axis=1, tiled=True).reshape(dp * tensor * rows, depth)

    def summed(weight):
        part = jnp.dot(block, weight, preferred_element_type=jnp.float32).astype(jnp.bfloat16)
        part = part.reshape(dp, tensor * rows, -1)
        got = lax.all_to_all(part, "dp", split_axis=0, concat_axis=0, tiled=False)
        return jnp.sum(got.astype(jnp.float32), axis=0)

    gate, up = summed(gate_weight), summed(up_weight)
    hidden = weights.astype(jnp.float32)[:, None] * jax.nn.silu(gate) * up
    return hidden.astype(jnp.bfloat16)


def order_of_planes(n):
    return [sorted(range(n), key=lambda other: (abs(other - plane), other)) for plane in range(n)]


def kernel(
    n,
    tok_ref,
    router_ref,
    ids_ref,
    gate_ref,
    up_ref,
    out_ref,
    w_buf,
    x_buf,
    share_buf,
    share_all,
    keep1,
    send1,
    recv1,
    keep2,
    send2,
    recv2,
    keep3,
    send3,
    recv3,
    load_sem,
    a_send,
    a_recv,
    z_up,
    z_down,
    z_recv,
    s_send,
    s_recv,
    c1_send,
    c1_recv,
    c2_send,
    c2_recv,
    c3_send,
    c3_recv,
):
    rows = tok_ref.shape[0]
    depth, width = gate_ref.shape
    me, plane = lax.axis_index("dp"), lax.axis_index("tensor")
    bits = [lax.rem(lax.div(me, m), 2) for m in (1, 2, 4)]

    def partner(mask):
        found = me
        for b, m in enumerate((1, 2, 4)):
            if mask & m:
                found = found + m * (1 - 2 * bits[b])
        return found

    def slot_of(mask):
        return (mask & 1) * 4 + (mask & 2) + (mask >> 2)

    loads = [
        pltpu.make_async_copy(ref, w_buf.at[i], load_sem.at[i])
        for i, ref in enumerate((gate_ref, up_ref))
    ]
    for load in loads:
        load.start()

    barrier = pltpu.get_barrier_semaphore()
    for mask in range(1, 8):
        pl.semaphore_signal(barrier, inc=1, device_id=(partner(mask), plane), device_id_type=MESH)
    for hop in range(1, n):
        pl.semaphore_signal(
            barrier, inc=1, device_id=(me, lax.rem(plane + hop, n)), device_id_type=MESH
        )
    pl.semaphore_wait(barrier, 7 + n - 1)

    spread = []
    for mask in (6, 4, 2, 7, 5, 3, 1):
        to = partner(mask)
        spread.append(
            pltpu.make_async_remote_copy(
                src_ref=tok_ref.at[:, pl.ds(pl.multiple_of(to * depth, depth), depth)],
                dst_ref=x_buf.at[plane, pl.ds(slot_of(mask) * rows, rows), :],
                send_sem=a_send.at[mask],
                recv_sem=a_recv.at[mask],
                device_id=(to, plane),
                device_id_type=MESH,
            )
        )
    for copy in spread:
        copy.start()
    x_buf[plane, 0:rows, :] = tok_ref[:, pl.ds(pl.multiple_of(me * depth, depth), depth)]

    def along(source, step, sem):
        return pltpu.make_async_remote_copy(
            src_ref=x_buf.at[source],
            dst_ref=x_buf.at[source],
            send_sem=sem.at[source],
            recv_sem=z_recv.at[source],
            device_id=(me, plane + step),
            device_id_type=MESH,
        )

    for copy in spread:
        copy.wait_recv()

    @pl.when(plane < n - 1)
    def _():
        along(plane, 1, z_up).start()

    @pl.when(plane > 0)
    def _():
        along(plane, -1, z_down).start()

    logits = lax.dot_general(
        router_ref[...],
        tok_ref[...],
        (((1,), (1,)), ((), ())),
        preferred_element_type=jnp.float32,
    )
    ids = ids_ref[...]
    first, second = ids[0:1, :], ids[1:2, :]
    routed = (first == 0) | (second == 0)
    other = jnp.where(first == 0, second, first)
    picked = lax.broadcasted_iota(jnp.int32, logits.shape, 0) == other
    other_logit = jnp.sum(jnp.where(picked, logits, 0.0), axis=0, keepdims=True)
    share = jnp.where(routed, jax.nn.sigmoid(logits[0:1, :] - other_logit), 0.0)
    square = (rows, rows)
    own = lax.broadcasted_iota(jnp.int32, square, 0) == lax.broadcasted_iota(jnp.int32, square, 1)
    column = jnp.sum(jnp.where(own, jnp.broadcast_to(share, square), 0.0), axis=1, keepdims=True)
    spread_share = jnp.broadcast_to(column, share_buf.shape).astype(share_buf.dtype)
    share_buf[...] = spread_share
    share_all[plane] = spread_share
    shares = [
        pltpu.make_async_remote_copy(
            src_ref=share_buf,
            dst_ref=share_all.at[plane],
            send_sem=s_send.at[hop],
            recv_sem=s_recv.at[hop],
            device_id=(me, lax.rem(plane + hop, n)),
            device_id_type=MESH,
        )
        for hop in range(1, n)
    ]
    for copy in shares:
        copy.start()

    table = order_of_planes(n)

    def source_of(k):
        found = plane
        for p in range(n):
            found = jnp.where(plane == p, table[p][k], found)
        return found

    def exchange(src, dst, send_sem, recv_sem, k, w, mask):
        return pltpu.make_async_remote_copy(
            src_ref=src.at[k, w],
            dst_ref=dst.at[k, w],
            send_sem=send_sem.at[k, w],
            recv_sem=recv_sem.at[k, w],
            device_id=(partner(mask), plane),
            device_id_type=MESH,
        )

    def over_core(k, w):
        return exchange(send1, recv1, c1_send, c1_recv, k, w, 1)

    def over_first(k, w):
        return exchange(send2, recv2, c2_send, c2_recv, k, w, (2, 4)[w])

    def over_second(k, w):
        return exchange(send3, recv3, c3_send, c3_recv, k, w, (4, 2)[w])

    tile = min(TILE, width)

    def multiply(k):
        source = source_of(k)
        for w in range(2):
            if k == 0:
                loads[w].wait()

            @pl.loop(0, width // tile)
            def _(i):
                columns = pl.ds(pl.multiple_of(i * tile, tile), tile)
                part = jnp.dot(
                    x_buf[source], w_buf[w, :, columns], preferred_element_type=jnp.float32
                )
                keep1[k, w, :, columns] = part[: 4 * rows]
                send1[k, w, :, columns] = part[4 * rows :]

            over_core(k, w).start()

    def after_core(k):
        for w in range(2):
            over_core(k, w).wait_recv()
            for xb in range(2):
                for yb in range(2):
                    at = pl.ds((xb * 2 + yb) * rows, rows)
                    total = keep1[k, w, at, :] + recv1[k, w, at, :]
                    leaves, place = ((xb, yb), (yb, xb))[w]
                    to = pl.ds(place * rows, rows)
                    if leaves:
                        send2[k, w, to, :] = total.astype(send2.dtype)
                    else:
                        keep2[k, w, to, :] = total
            over_first(k, w).start()

    def after_first(k):
        for w in range(2):
            over_first(k, w).wait_recv()
            leave, stay = pl.ds(rows, rows), pl.ds(0, rows)
            send3[k, w] = (
                keep2[k, w, leave, :] + recv2[k, w, leave, :].astype(jnp.float32)
            ).astype(send3.dtype)
            over_second(k, w).start()
            keep3[k, w] = keep2[k, w, stay, :] + recv2[k, w, stay, :].astype(jnp.float32)

    def finish(k):
        source = source_of(k)
        for w in range(2):
            over_second(k, w).wait_recv()
        gate = keep3[k, 0] + recv3[k, 0].astype(jnp.float32)
        up = keep3[k, 1] + recv3[k, 1].astype(jnp.float32)
        part = share_all[source][:, 0:1].astype(jnp.float32)
        hidden = part * (gate * jax.nn.sigmoid(gate)) * up
        out_ref[pl.ds(pl.multiple_of(source * rows, rows), rows), :] = hidden.astype(out_ref.dtype)

    for k in range(n):
        if k:

            @pl.when(plane - k >= 0)
            def _():
                along(plane - k, 1, z_up).wait_recv()

            @pl.when((plane - k >= 0) & (plane < n - 1))
            def _():
                along(plane - k, 1, z_up).start()

            @pl.when(plane + k < n)
            def _():
                along(plane + k, -1, z_down).wait_recv()

            @pl.when((plane + k < n) & (plane > 0))
            def _():
                along(plane + k, -1, z_down).start()

        multiply(k)
        if k >= 1:
            after_first(k - 1)
        after_core(k)
        if k == 2:
            for copy in shares:
                copy.wait_recv()
        if k >= 2:
            finish(k - 2)
    after_first(n - 1)
    finish(n - 2)
    finish(n - 1)

    for copy in spread + shares:
        copy.wait_send()
    for p in range(n):

        @pl.when((plane >= p) & (plane < n - 1))
        def _():
            along(p, 1, z_up).wait_send()

        @pl.when((plane <= p) & (plane > 0))
        def _():
            along(p, -1, z_down).wait_send()

    for k in range(n):
        for w in range(2):
            over_core(k, w).wait_send()
            over_first(k, w).wait_send()
            over_second(k, w).wait_send()


def one_kernel(mesh, tokens, router_weight, expert_ids, gate_weight, up_weight):
    n = mesh.shape["tensor"]
    rows = tokens.shape[0]
    depth, width = gate_weight.shape
    f32, bf16 = jnp.float32, jnp.bfloat16
    dma = pltpu.SemaphoreType.DMA
    vmem = pl.BlockSpec(memory_space=pltpu.VMEM)
    hbm = pl.BlockSpec(memory_space=pl.ANY)
    return pl.pallas_call(
        functools.partial(kernel, n),
        out_shape=jax.ShapeDtypeStruct((n * rows, width), bf16),
        in_specs=[vmem, vmem, vmem, hbm, hbm],
        out_specs=vmem,
        scratch_shapes=[
            pltpu.VMEM((2, depth, width), bf16),
            pltpu.VMEM((n, 8 * rows, depth), bf16),
            pltpu.VMEM((rows, 128), bf16),
            pltpu.VMEM((n, rows, 128), bf16),
            pltpu.VMEM((n, 2, 4 * rows, width), f32),
            pltpu.VMEM((n, 2, 4 * rows, width), f32),
            pltpu.VMEM((n, 2, 4 * rows, width), f32),
            pltpu.VMEM((n, 2, 2 * rows, width), f32),
            pltpu.VMEM((n, 2, 2 * rows, width), bf16),
            pltpu.VMEM((n, 2, 2 * rows, width), bf16),
            pltpu.VMEM((n, 2, rows, width), f32),
            pltpu.VMEM((n, 2, rows, width), bf16),
            pltpu.VMEM((n, 2, rows, width), bf16),
            dma((2,)),
            dma((8,)),
            dma((8,)),
            dma((n,)),
            dma((n,)),
            dma((n,)),
            dma((n,)),
            dma((n,)),
            dma((n, 2)),
            dma((n, 2)),
            dma((n, 2)),
            dma((n, 2)),
            dma((n, 2)),
            dma((n, 2)),
        ],
        compiler_params=pltpu.CompilerParams(
            collective_id=0, has_side_effects=True, vmem_limit_bytes=58 * 2**20
        ),
        cost_estimate=pl.CostEstimate(
            flops=2 * n * 8 * rows * depth * 2 * width,
            bytes_accessed=2 * depth * width * 2,
            transcendentals=n * rows * width,
        ),
    )(tokens, router_weight.T, expert_ids.T, gate_weight, up_weight)


def solution(mesh):
    chosen = one_kernel if mesh.shape["dp"] == 8 and mesh.shape["tensor"] == 4 else stationary_weights

    def per_device(*args):
        return chosen(mesh, *args)

    return jax.shard_map(
        per_device,
        mesh=mesh,
        in_specs=(
            P(("dp", "tensor"), None),
            P(),
            P(("dp", "tensor"), None),
            P("dp", "tensor"),
            P("dp", "tensor"),
        ),
        out_specs=P("dp", "tensor"),
        check_vma=False,
    )
```

```python
import functools

import jax
import jax.numpy as jnp
from jax import lax
from jax.experimental import pallas as pl
from jax.experimental.pallas import tpu as pltpu
from jax.sharding import PartitionSpec as P

MESH = pl.DeviceIdType.MESH
TILE = 512


def share_of_expert(tokens, router_weight, expert_ids):
    logits = jnp.dot(tokens, router_weight, preferred_element_type=jnp.float32)
    first_zero = expert_ids[:, 0] == 0
    routed = first_zero | (expert_ids[:, 1] == 0)
    other = jnp.where(first_zero, expert_ids[:, 1], expert_ids[:, 0])
    picked = jnp.arange(logits.shape[1], dtype=jnp.int32)[None, :] == other[:, None]
    other_logit = jnp.sum(jnp.where(picked, logits, jnp.float32(0.0)), axis=1)
    return jnp.where(routed, jax.nn.sigmoid(logits[:, 0] - other_logit), jnp.float32(0.0)).astype(
        jnp.bfloat16
    )


def stationary_weights(mesh, tokens, router_weight, expert_ids, gate_weight, up_weight):
    dp, tensor = mesh.shape["dp"], mesh.shape["tensor"]
    rows, depth = tokens.shape[0], gate_weight.shape[0]
    weights = lax.all_gather(
        share_of_expert(tokens, router_weight, expert_ids), "tensor", axis=0, tiled=True
    )
    columns = lax.all_to_all(
        tokens.reshape(rows, dp, depth), "dp", split_axis=1, concat_axis=0, tiled=False
    )
    block = lax.all_gather(columns, "tensor", axis=1, tiled=True).reshape(dp * tensor * rows, depth)

    def summed(weight):
        part = jnp.dot(block, weight, preferred_element_type=jnp.float32).astype(jnp.bfloat16)
        part = part.reshape(dp, tensor * rows, -1)
        got = lax.all_to_all(part, "dp", split_axis=0, concat_axis=0, tiled=False)
        return jnp.sum(got.astype(jnp.float32), axis=0)

    gate, up = summed(gate_weight), summed(up_weight)
    hidden = weights.astype(jnp.float32)[:, None] * jax.nn.silu(gate) * up
    return hidden.astype(jnp.bfloat16)


def order_of_planes(n):
    return [sorted(range(n), key=lambda other: (abs(other - plane), other)) for plane in range(n)]


def kernel(
    n,
    tok_ref,
    router_ref,
    ids_ref,
    gate_ref,
    up_ref,
    out_ref,
    tok_buf,
    router_buf,
    w_buf,
    x_buf,
    share_buf,
    share_all,
    keep1,
    send1,
    recv1,
    keep2,
    send2,
    recv2,
    keep3,
    send3,
    recv3,
    load_sem,
    a_send,
    a_recv,
    z_up,
    z_down,
    z_recv,
    s_send,
    s_recv,
    c1_send,
    c1_recv,
    c2_send,
    c2_recv,
    c3_send,
    c3_recv,
):
    rows = tok_ref.shape[0]
    depth, width = gate_ref.shape
    me, plane = lax.axis_index("dp"), lax.axis_index("tensor")
    bits = [lax.rem(lax.div(me, m), 2) for m in (1, 2, 4)]

    def partner(mask):
        found = me
        for b, m in enumerate((1, 2, 4)):
            if mask & m:
                found = found + m * (1 - 2 * bits[b])
        return found

    def slot_of(mask):
        return (mask & 1) * 4 + (mask & 2) + (mask >> 2)

    def columns_of(device):
        return tok_ref.at[:, pl.ds(pl.multiple_of(device * depth, depth), depth)]

    loads = [
        pltpu.make_async_copy(src, dst, load_sem.at[i])
        for i, (src, dst) in enumerate(
            (
                (gate_ref, w_buf.at[0]),
                (up_ref, w_buf.at[1]),
                (tok_ref, tok_buf),
                (router_ref, router_buf),
                (columns_of(me), x_buf.at[plane, pl.ds(0, rows), :]),
            )
        )
    ]
    for i in (4, 2, 3, 0, 1):
        loads[i].start()

    barrier = pltpu.get_barrier_semaphore()
    for mask in range(1, 8):
        pl.semaphore_signal(barrier, inc=1, device_id=(partner(mask), plane), device_id_type=MESH)
    for hop in range(1, n):
        pl.semaphore_signal(
            barrier, inc=1, device_id=(me, lax.rem(plane + hop, n)), device_id_type=MESH
        )
    pl.semaphore_wait(barrier, 7 + n - 1)

    spread = []
    for mask in (6, 4, 2, 7, 5, 3, 1):
        to = partner(mask)
        spread.append(
            pltpu.make_async_remote_copy(
                src_ref=columns_of(to),
                dst_ref=x_buf.at[plane, pl.ds(slot_of(mask) * rows, rows), :],
                send_sem=a_send.at[mask],
                recv_sem=a_recv.at[mask],
                device_id=(to, plane),
                device_id_type=MESH,
            )
        )
    for copy in spread:
        copy.start()

    def along(source, half, step, sem):
        part = pl.ds(half * 4 * rows, 4 * rows)
        return pltpu.make_async_remote_copy(
            src_ref=x_buf.at[source, part, :],
            dst_ref=x_buf.at[source, part, :],
            send_sem=sem.at[source, half],
            recv_sem=z_recv.at[source, half],
            device_id=(me, plane + step),
            device_id_type=MESH,
        )

    loads[4].wait()
    for half in range(2):
        for copy in spread[3 * half : 3 + 4 * half]:
            copy.wait_recv()

        @pl.when(plane < n - 1)
        def _():
            along(plane, half, 1, z_up).start()

        @pl.when(plane > 0)
        def _():
            along(plane, half, -1, z_down).start()

    def pass_on(k, half):
        @pl.when((plane - k >= 0) & (plane < n - 1))
        def _():
            along(plane - k, half, 1, z_up).wait_recv()
            along(plane - k, half, 1, z_up).start()

        @pl.when((plane + k < n) & (plane > 0))
        def _():
            along(plane + k, half, -1, z_down).wait_recv()
            along(plane + k, half, -1, z_down).start()

    def take(k, half):
        @pl.when((plane - k >= 0) & (plane == n - 1))
        def _():
            along(plane - k, half, 1, z_up).wait_recv()

        @pl.when((plane + k < n) & (plane == 0))
        def _():
            along(plane + k, half, -1, z_down).wait_recv()

    loads[2].wait()
    loads[3].wait()
    logits = lax.dot_general(
        router_buf[...],
        tok_buf[...],
        (((1,), (1,)), ((), ())),
        preferred_element_type=jnp.float32,
    )
    ids = ids_ref[...]
    first, second = ids[0:1, :], ids[1:2, :]
    routed = (first == 0) | (second == 0)
    other = jnp.where(first == 0, second, first)
    picked = lax.broadcasted_iota(jnp.int32, logits.shape, 0) == other
    other_logit = jnp.sum(jnp.where(picked, logits, 0.0), axis=0, keepdims=True)
    share = jnp.where(routed, jax.nn.sigmoid(logits[0:1, :] - other_logit), 0.0)
    square = (rows, rows)
    own = lax.broadcasted_iota(jnp.int32, square, 0) == lax.broadcasted_iota(jnp.int32, square, 1)
    column = jnp.sum(jnp.where(own, jnp.broadcast_to(share, square), 0.0), axis=1, keepdims=True)
    spread_share = jnp.broadcast_to(column, share_buf.shape).astype(share_buf.dtype)
    share_buf[...] = spread_share
    share_all[plane] = spread_share
    shares = [
        pltpu.make_async_remote_copy(
            src_ref=share_buf,
            dst_ref=share_all.at[plane],
            send_sem=s_send.at[hop],
            recv_sem=s_recv.at[hop],
            device_id=(me, lax.rem(plane + hop, n)),
            device_id_type=MESH,
        )
        for hop in range(1, n)
    ]
    for copy in shares:
        copy.start()

    table = order_of_planes(n)

    def source_of(k):
        found = plane
        for p in range(n):
            found = jnp.where(plane == p, table[p][k], found)
        return found

    def exchange(src, dst, send_sem, recv_sem, k, w, mask):
        return pltpu.make_async_remote_copy(
            src_ref=src.at[k, w],
            dst_ref=dst.at[k, w],
            send_sem=send_sem.at[k, w],
            recv_sem=recv_sem.at[k, w],
            device_id=(partner(mask), plane),
            device_id_type=MESH,
        )

    def over_core(k, w):
        return exchange(send1, recv1, c1_send, c1_recv, k, w, 1)

    def over_first(k, w):
        return exchange(send2, recv2, c2_send, c2_recv, k, w, (2, 4)[w])

    def over_second(k, w):
        return exchange(send3, recv3, c3_send, c3_recv, k, w, (4, 2)[w])

    tile = min(TILE, width)

    def multiply(k):
        source = source_of(k)
        for w in range(2):
            if k == 0:
                loads[w].wait()

            @pl.loop(0, width // tile)
            def _(i):
                columns = pl.ds(pl.multiple_of(i * tile, tile), tile)
                part = jnp.dot(
                    x_buf[source], w_buf[w, :, columns], preferred_element_type=jnp.float32
                )
                keep1[k, w, :, columns] = part[: 4 * rows]
                send1[k, w, :, columns] = part[4 * rows :]

            over_core(k, w).start()

    def after_core(k):
        for w in range(2):
            over_core(k, w).wait_recv()
            for xb in range(2):
                for yb in range(2):
                    at = pl.ds((xb * 2 + yb) * rows, rows)
                    total = keep1[k, w, at, :] + recv1[k, w, at, :]
                    leaves, place = ((xb, yb), (yb, xb))[w]
                    to = pl.ds(place * rows, rows)
                    if leaves:
                        send2[k, w, to, :] = total.astype(send2.dtype)
                    else:
                        keep2[k, w, to, :] = total
            over_first(k, w).start()

    def after_first(k):
        for w in range(2):
            over_first(k, w).wait_recv()
            leave, stay = pl.ds(rows, rows), pl.ds(0, rows)
            send3[k, w] = (
                keep2[k, w, leave, :] + recv2[k, w, leave, :].astype(jnp.float32)
            ).astype(send3.dtype)
            over_second(k, w).start()
            keep3[k, w] = keep2[k, w, stay, :] + recv2[k, w, stay, :].astype(jnp.float32)

    def finish(k):
        source = source_of(k)
        for w in range(2):
            over_second(k, w).wait_recv()
        gate = keep3[k, 0] + recv3[k, 0].astype(jnp.float32)
        up = keep3[k, 1] + recv3[k, 1].astype(jnp.float32)
        part = share_all[source][:, 0:1].astype(jnp.float32)
        hidden = part * (gate * jax.nn.sigmoid(gate)) * up
        out_ref[pl.ds(pl.multiple_of(source * rows, rows), rows), :] = hidden.astype(out_ref.dtype)

    for k in range(n):
        if k:
            pass_on(k, 1)
            take(k, 0)
            take(k, 1)
        multiply(k)
        if k + 1 < n:
            pass_on(k + 1, 0)
        if k >= 2:
            after_first(k - 2)
        after_core(k)
    for copy in shares:
        copy.wait_recv()
    for k in range(n):
        if k >= n - 2:
            after_first(k)
        if k == n - 2:
            for done in range(n - 2):
                finish(done)
    finish(n - 2)
    finish(n - 1)

    for copy in spread + shares:
        copy.wait_send()
    for p in range(n):

        @pl.when((plane >= p) & (plane < n - 1))
        def _():
            for half in range(2):
                along(p, half, 1, z_up).wait_send()

        @pl.when((plane <= p) & (plane > 0))
        def _():
            for half in range(2):
                along(p, half, -1, z_down).wait_send()

    for k in range(n):
        for w in range(2):
            over_core(k, w).wait_send()
            over_first(k, w).wait_send()
            over_second(k, w).wait_send()


def one_kernel(mesh, tokens, router_weight, expert_ids, gate_weight, up_weight):
    n = mesh.shape["tensor"]
    rows = tokens.shape[0]
    depth, width = gate_weight.shape
    f32, bf16 = jnp.float32, jnp.bfloat16
    dma = pltpu.SemaphoreType.DMA
    vmem = pl.BlockSpec(memory_space=pltpu.VMEM)
    hbm = pl.BlockSpec(memory_space=pl.ANY)
    return pl.pallas_call(
        functools.partial(kernel, n),
        out_shape=jax.ShapeDtypeStruct((n * rows, width), bf16),
        in_specs=[hbm, hbm, vmem, hbm, hbm],
        out_specs=vmem,
        scratch_shapes=[
            pltpu.VMEM(tokens.shape, bf16),
            pltpu.VMEM(router_weight.shape[::-1], bf16),
            pltpu.VMEM((2, depth, width), bf16),
            pltpu.VMEM((n, 8 * rows, depth), bf16),
            pltpu.VMEM((rows, 128), bf16),
            pltpu.VMEM((n, rows, 128), bf16),
            pltpu.VMEM((n, 2, 4 * rows, width), f32),
            pltpu.VMEM((n, 2, 4 * rows, width), f32),
            pltpu.VMEM((n, 2, 4 * rows, width), f32),
            pltpu.VMEM((n, 2, 2 * rows, width), f32),
            pltpu.VMEM((n, 2, 2 * rows, width), bf16),
            pltpu.VMEM((n, 2, 2 * rows, width), bf16),
            pltpu.VMEM((n, 2, rows, width), f32),
            pltpu.VMEM((n, 2, rows, width), bf16),
            pltpu.VMEM((n, 2, rows, width), bf16),
            dma((5,)),
            dma((8,)),
            dma((8,)),
            dma((n, 2)),
            dma((n, 2)),
            dma((n, 2)),
            dma((n,)),
            dma((n,)),
            dma((n, 2)),
            dma((n, 2)),
            dma((n, 2)),
            dma((n, 2)),
            dma((n, 2)),
            dma((n, 2)),
        ],
        compiler_params=pltpu.CompilerParams(
            collective_id=0, has_side_effects=True, vmem_limit_bytes=63_300_000
        ),
        cost_estimate=pl.CostEstimate(
            flops=2 * n * 8 * rows * depth * 2 * width,
            bytes_accessed=2 * depth * width * 2,
            transcendentals=n * rows * width,
        ),
    )(tokens, router_weight.T, expert_ids.T, gate_weight, up_weight)


def solution(mesh):
    chosen = one_kernel if mesh.shape["dp"] == 8 and mesh.shape["tensor"] == 4 else stationary_weights

    def per_device(*args):
        return chosen(mesh, *args)

    return jax.shard_map(
        per_device,
        mesh=mesh,
        in_specs=(
            P(("dp", "tensor"), None),
            P(),
            P(("dp", "tensor"), None),
            P("dp", "tensor"),
            P("dp", "tensor"),
        ),
        out_specs=P("dp", "tensor"),
        check_vma=False,
    )
```

```python
import functools

import jax
import jax.numpy as jnp
from jax import lax
from jax.experimental import pallas as pl
from jax.experimental.pallas import tpu as pltpu
from jax.sharding import PartitionSpec as P

MESH = pl.DeviceIdType.MESH
PARTS = 2


def share_of_expert(tokens, router_weight, expert_ids):
    logits = jnp.dot(tokens, router_weight, preferred_element_type=jnp.float32)
    first_zero = expert_ids[:, 0] == 0
    routed = first_zero | (expert_ids[:, 1] == 0)
    other = jnp.where(first_zero, expert_ids[:, 1], expert_ids[:, 0])
    picked = jnp.arange(logits.shape[1], dtype=jnp.int32)[None, :] == other[:, None]
    other_logit = jnp.sum(jnp.where(picked, logits, jnp.float32(0.0)), axis=1)
    return jnp.where(routed, jax.nn.sigmoid(logits[:, 0] - other_logit), jnp.float32(0.0)).astype(
        jnp.bfloat16
    )


def stationary_weights(mesh, tokens, router_weight, expert_ids, gate_weight, up_weight):
    dp, tensor = mesh.shape["dp"], mesh.shape["tensor"]
    rows, depth = tokens.shape[0], gate_weight.shape[0]
    weights = lax.all_gather(
        share_of_expert(tokens, router_weight, expert_ids), "tensor", axis=0, tiled=True
    )
    columns = lax.all_to_all(
        tokens.reshape(rows, dp, depth), "dp", split_axis=1, concat_axis=0, tiled=False
    )
    block = lax.all_gather(columns, "tensor", axis=1, tiled=True).reshape(dp * tensor * rows, depth)

    def summed(weight):
        part = jnp.dot(block, weight, preferred_element_type=jnp.float32).astype(jnp.bfloat16)
        part = part.reshape(dp, tensor * rows, -1)
        got = lax.all_to_all(part, "dp", split_axis=0, concat_axis=0, tiled=False)
        return jnp.sum(got.astype(jnp.float32), axis=0)

    gate, up = summed(gate_weight), summed(up_weight)
    hidden = weights.astype(jnp.float32)[:, None] * jax.nn.silu(gate) * up
    return hidden.astype(jnp.bfloat16)


def order_of_planes(n):
    return [sorted(range(n), key=lambda other: (abs(other - plane), other)) for plane in range(n)]


def kernel(
    n,
    tok_ref,
    router_ref,
    ids_ref,
    gate_ref,
    up_ref,
    out_ref,
    tok_buf,
    router_buf,
    w_buf,
    x_buf,
    share_buf,
    share_all,
    keep1,
    send1,
    recv1,
    keep2,
    send2,
    recv2,
    keep3,
    send3,
    recv3,
    load_sem,
    a_send,
    a_recv,
    z_up,
    z_down,
    z_recv,
    s_send,
    s_recv,
    c1_send,
    c1_recv,
    c2_send,
    c2_recv,
    c3_send,
    c3_recv,
):
    rows = tok_ref.shape[0]
    depth, width = gate_ref.shape
    me, plane = lax.axis_index("dp"), lax.axis_index("tensor")
    bits = [lax.rem(lax.div(me, m), 2) for m in (1, 2, 4)]

    def partner(mask):
        found = me
        for b, m in enumerate((1, 2, 4)):
            if mask & m:
                found = found + m * (1 - 2 * bits[b])
        return found

    def slot_of(mask):
        return (mask & 1) * 4 + (mask & 2) + (mask >> 2)

    def columns_of(device):
        return tok_ref.at[:, pl.ds(pl.multiple_of(device * depth, depth), depth)]

    loads = [
        pltpu.make_async_copy(src, dst, load_sem.at[i])
        for i, (src, dst) in enumerate(
            (
                (gate_ref, w_buf.at[0]),
                (up_ref, w_buf.at[1]),
                (tok_ref, tok_buf),
                (router_ref, router_buf),
                (columns_of(me), x_buf.at[plane, pl.ds(0, rows), :]),
            )
        )
    ]
    for i in (4, 2, 3, 0, 1):
        loads[i].start()

    barrier = pltpu.get_barrier_semaphore()
    for mask in range(1, 8):
        pl.semaphore_signal(barrier, inc=1, device_id=(partner(mask), plane), device_id_type=MESH)
    for hop in range(1, n):
        pl.semaphore_signal(
            barrier, inc=1, device_id=(me, lax.rem(plane + hop, n)), device_id_type=MESH
        )
    pl.semaphore_wait(barrier, 7 + n - 1)

    spread = []
    for mask in (6, 4, 2, 7, 5, 3, 1):
        to = partner(mask)
        spread.append(
            pltpu.make_async_remote_copy(
                src_ref=columns_of(to),
                dst_ref=x_buf.at[plane, pl.ds(slot_of(mask) * rows, rows), :],
                send_sem=a_send.at[mask],
                recv_sem=a_recv.at[mask],
                device_id=(to, plane),
                device_id_type=MESH,
            )
        )
    for copy in spread:
        copy.start()

    def along(source, half, step, sem):
        part = pl.ds(half * 4 * rows, 4 * rows)
        return pltpu.make_async_remote_copy(
            src_ref=x_buf.at[source, part, :],
            dst_ref=x_buf.at[source, part, :],
            send_sem=sem.at[source, half],
            recv_sem=z_recv.at[source, half],
            device_id=(me, plane + step),
            device_id_type=MESH,
        )

    loads[4].wait()
    for half in range(2):
        for copy in spread[3 * half : 3 + 4 * half]:
            copy.wait_recv()

        @pl.when(plane < n - 1)
        def _():
            along(plane, half, 1, z_up).start()

        @pl.when(plane > 0)
        def _():
            along(plane, half, -1, z_down).start()

    def pass_on(k, half):
        @pl.when((plane - k >= 0) & (plane < n - 1))
        def _():
            along(plane - k, half, 1, z_up).wait_recv()
            along(plane - k, half, 1, z_up).start()

        @pl.when((plane + k < n) & (plane > 0))
        def _():
            along(plane + k, half, -1, z_down).wait_recv()
            along(plane + k, half, -1, z_down).start()

    def take(k, half):
        @pl.when((plane - k >= 0) & (plane == n - 1))
        def _():
            along(plane - k, half, 1, z_up).wait_recv()

        @pl.when((plane + k < n) & (plane == 0))
        def _():
            along(plane + k, half, -1, z_down).wait_recv()

    loads[2].wait()
    loads[3].wait()
    logits = lax.dot_general(
        router_buf[...],
        tok_buf[...],
        (((1,), (1,)), ((), ())),
        preferred_element_type=jnp.float32,
    )
    ids = ids_ref[...]
    first, second = ids[0:1, :], ids[1:2, :]
    routed = (first == 0) | (second == 0)
    other = jnp.where(first == 0, second, first)
    picked = lax.broadcasted_iota(jnp.int32, logits.shape, 0) == other
    other_logit = jnp.sum(jnp.where(picked, logits, 0.0), axis=0, keepdims=True)
    share = jnp.where(routed, jax.nn.sigmoid(logits[0:1, :] - other_logit), 0.0)
    square = (rows, rows)
    own = lax.broadcasted_iota(jnp.int32, square, 0) == lax.broadcasted_iota(jnp.int32, square, 1)
    column = jnp.sum(jnp.where(own, jnp.broadcast_to(share, square), 0.0), axis=1, keepdims=True)
    spread_share = jnp.broadcast_to(column, share_buf.shape).astype(share_buf.dtype)
    share_buf[...] = spread_share
    share_all[plane] = spread_share
    shares = [
        pltpu.make_async_remote_copy(
            src_ref=share_buf,
            dst_ref=share_all.at[plane],
            send_sem=s_send.at[hop],
            recv_sem=s_recv.at[hop],
            device_id=(me, lax.rem(plane + hop, n)),
            device_id_type=MESH,
        )
        for hop in range(1, n)
    ]
    for copy in shares:
        copy.start()

    table = order_of_planes(n)

    def source_of(k):
        found = plane
        for p in range(n):
            found = jnp.where(plane == p, table[p][k], found)
        return found

    def exchange(src, dst, send_sem, recv_sem, k, w, mask):
        return pltpu.make_async_remote_copy(
            src_ref=src.at[k, w],
            dst_ref=dst.at[k, w],
            send_sem=send_sem.at[k, w],
            recv_sem=recv_sem.at[k, w],
            device_id=(partner(mask), plane),
            device_id_type=MESH,
        )

    def over_core(k, w):
        return exchange(send1, recv1, c1_send, c1_recv, k, w, 1)

    def over_first(k, w):
        return exchange(send2, recv2, c2_send, c2_recv, k, w, (2, 4)[w % 2])

    def over_second(k, w):
        return exchange(send3, recv3, c3_send, c3_recv, k, w, (4, 2)[w % 2])

    tile = width // PARTS
    units = 2 * PARTS

    def multiply(k):
        source = source_of(k)
        for w in range(units):
            if k == 0 and w < 2:
                loads[w].wait()
            columns = pl.ds(w // 2 * tile, tile)
            part = jnp.dot(
                x_buf[source], w_buf[w % 2, :, columns], preferred_element_type=jnp.float32
            )
            keep1[k, w] = part[: 4 * rows]
            send1[k, w] = part[4 * rows :]
            over_core(k, w).start()

    def after_core(k):
        for w in range(units):
            over_core(k, w).wait_recv()
            for xb in range(2):
                for yb in range(2):
                    at = pl.ds((xb * 2 + yb) * rows, rows)
                    total = keep1[k, w, at, :] + recv1[k, w, at, :]
                    leaves, place = ((xb, yb), (yb, xb))[w % 2]
                    to = pl.ds(place * rows, rows)
                    if leaves:
                        send2[k, w, to, :] = total.astype(send2.dtype)
                    else:
                        keep2[k, w, to, :] = total
            over_first(k, w).start()

    def after_first(k):
        for w in range(units):
            over_first(k, w).wait_recv()
            leave, stay = pl.ds(rows, rows), pl.ds(0, rows)
            send3[k, w] = (
                keep2[k, w, leave, :] + recv2[k, w, leave, :].astype(jnp.float32)
            ).astype(send3.dtype)
            over_second(k, w).start()
            keep3[k, w] = keep2[k, w, stay, :] + recv2[k, w, stay, :].astype(jnp.float32)

    def finish(k):
        source = source_of(k)
        for w in range(0, units, 2):
            over_second(k, w).wait_recv()
            over_second(k, w + 1).wait_recv()
            gate = keep3[k, w] + recv3[k, w].astype(jnp.float32)
            up = keep3[k, w + 1] + recv3[k, w + 1].astype(jnp.float32)
            share_of_row = share_all[source][:, 0:1].astype(jnp.float32)
            hidden = share_of_row * (gate * jax.nn.sigmoid(gate)) * up
            out_ref[
                pl.ds(pl.multiple_of(source * rows, rows), rows), pl.ds(w // 2 * tile, tile)
            ] = hidden.astype(out_ref.dtype)

    for k in range(n):
        if k:
            pass_on(k, 1)
            take(k, 0)
            take(k, 1)
        multiply(k)
        if k + 1 < n:
            pass_on(k + 1, 0)
        after_core(k)
        if k >= 1:
            after_first(k - 1)
    for copy in shares:
        copy.wait_recv()
    for k in range(n):
        if k >= n - 1:
            after_first(k)
        if k == n - 2:
            for done in range(n - 2):
                finish(done)
    finish(n - 2)
    finish(n - 1)

    for copy in spread + shares:
        copy.wait_send()
    for p in range(n):

        @pl.when((plane >= p) & (plane < n - 1))
        def _():
            for half in range(2):
                along(p, half, 1, z_up).wait_send()

        @pl.when((plane <= p) & (plane > 0))
        def _():
            for half in range(2):
                along(p, half, -1, z_down).wait_send()

    for k in range(n):
        for w in range(units):
            over_core(k, w).wait_send()
            over_first(k, w).wait_send()
            over_second(k, w).wait_send()


def one_kernel(mesh, tokens, router_weight, expert_ids, gate_weight, up_weight):
    n = mesh.shape["tensor"]
    rows = tokens.shape[0]
    depth, width = gate_weight.shape
    f32, bf16 = jnp.float32, jnp.bfloat16
    dma = pltpu.SemaphoreType.DMA
    vmem = pl.BlockSpec(memory_space=pltpu.VMEM)
    hbm = pl.BlockSpec(memory_space=pl.ANY)
    return pl.pallas_call(
        functools.partial(kernel, n),
        out_shape=jax.ShapeDtypeStruct((n * rows, width), bf16),
        in_specs=[hbm, hbm, vmem, hbm, hbm],
        out_specs=vmem,
        scratch_shapes=[
            pltpu.VMEM(tokens.shape, bf16),
            pltpu.VMEM(router_weight.shape[::-1], bf16),
            pltpu.VMEM((2, depth, width), bf16),
            pltpu.VMEM((n, 8 * rows, depth), bf16),
            pltpu.VMEM((rows, 128), bf16),
            pltpu.VMEM((n, rows, 128), bf16),
            pltpu.VMEM((n, 2 * PARTS, 4 * rows, width // PARTS), f32),
            pltpu.VMEM((n, 2 * PARTS, 4 * rows, width // PARTS), f32),
            pltpu.VMEM((n, 2 * PARTS, 4 * rows, width // PARTS), f32),
            pltpu.VMEM((n, 2 * PARTS, 2 * rows, width // PARTS), f32),
            pltpu.VMEM((n, 2 * PARTS, 2 * rows, width // PARTS), bf16),
            pltpu.VMEM((n, 2 * PARTS, 2 * rows, width // PARTS), bf16),
            pltpu.VMEM((n, 2 * PARTS, rows, width // PARTS), f32),
            pltpu.VMEM((n, 2 * PARTS, rows, width // PARTS), bf16),
            pltpu.VMEM((n, 2 * PARTS, rows, width // PARTS), bf16),
            dma((5,)),
            dma((8,)),
            dma((8,)),
            dma((n, 2)),
            dma((n, 2)),
            dma((n, 2)),
            dma((n,)),
            dma((n,)),
            dma((n, 2 * PARTS)),
            dma((n, 2 * PARTS)),
            dma((n, 2 * PARTS)),
            dma((n, 2 * PARTS)),
            dma((n, 2 * PARTS)),
            dma((n, 2 * PARTS)),
        ],
        compiler_params=pltpu.CompilerParams(
            collective_id=0, has_side_effects=True, vmem_limit_bytes=63_300_000
        ),
        cost_estimate=pl.CostEstimate(
            flops=2 * n * 8 * rows * depth * 2 * width,
            bytes_accessed=2 * depth * width * 2,
            transcendentals=n * rows * width,
        ),
    )(tokens, router_weight.T, expert_ids.T, gate_weight, up_weight)


def solution(mesh):
    chosen = one_kernel if mesh.shape["dp"] == 8 and mesh.shape["tensor"] == 4 else stationary_weights

    def per_device(*args):
        return chosen(mesh, *args)

    return jax.shard_map(
        per_device,
        mesh=mesh,
        in_specs=(
            P(("dp", "tensor"), None),
            P(),
            P(("dp", "tensor"), None),
            P("dp", "tensor"),
            P("dp", "tensor"),
        ),
        out_specs=P("dp", "tensor"),
        check_vma=False,
    )
```
